256 devices in a mesh: ex: 32 (over x_lo, z, core), layer: 8 (over x_hi, y).
Axes of the slice: x: 4 (x_hi: 2, x_lo: 2; x = x_hi * 2 + x_lo), y: 4, z: 8, core: 2. Of those that a mesh axis runs over, the one named last changes fastest.
Arguments:
- activations: bfloat16 [8, 64, 256, 11008], P('layer', 'ex'), may hold values from -6 to 6
- grad_proj: float32 [8, 64, 64, 256], P('layer', 'ex'), may hold values from -6 to 6
- proj_in: bfloat16 [8, 64, 11008], P('layer'), may hold values from -0.0546875 to 0.0546875
Outputs:
- gram: float32 [64, 64], P('ex', 'layer')
The draws below stay inside these ranges and needn't reach their ends.
All inputs are finite; a program needn't handle non-finite values.
Results may differ from the reference program's by a relative error of at most 0.0003.
Values sent between devices are 32-bit elements; how exact they have to be, the bound alone decides.
No kernel may reach another device: no remote copies, remote signals or barrier semaphores. Data moves between devices by JAX's collectives and lax.ppermute only.
A program may use at most 64 MiB of HBM per device.

```python
import math
import jax
import jax.numpy as jnp
from jax import lax

FF = 11008
RANK = 64
SEQ = 256
EXAMPLES = 64
LAYERS = 8


def block_levels(stream_key, extent, split, least, top_value):
    def one(axis_at, parts):
        heights = jax.random.uniform(jax.random.fold_in(jax.random.fold_in(stream_key, 6), axis_at), (parts,), jnp.float32, least / len(split), top_value / len(split))
        return jnp.repeat(jnp.exp(heights), extent[axis_at] // parts).reshape((-1,) + (1,) * (len(extent) - axis_at - 1))

    factor_of = one(*split[0])
    for cut in split[1:]:
        factor_of = factor_of * one(*cut)
    return factor_of


def noise(stream_key, dims, deviation, limit, pieces=(), kind=jnp.bfloat16):
    array = deviation * jax.random.normal(stream_key, dims, jnp.float32)
    if pieces:
        array = array * block_levels(stream_key, dims, pieces, -0.22, 0.18)
    return jnp.clip(array, -limit, limit).astype(kind)


def setup_inputs(seed: int = 0) -> dict:
    key_list = jax.random.split(jax.random.key(seed), 4)
    return {
        "activations": noise(key_list[0], (LAYERS, EXAMPLES, SEQ, FF), 1.0, 6.0, ((0, 8), (1, 32))),
        "grad_proj": noise(key_list[1], (LAYERS, EXAMPLES, RANK, SEQ), 1.0, 6.0, ((0, 8), (1, 32)), jnp.float32),
        "proj_in": noise(key_list[2], (LAYERS, RANK, FF), FF ** -0.5, 0.0546875, ((0, 8),)),
    }


def layer_features(acts, grads, factor):
    flat = acts.reshape(-1, acts.shape[-1])
    px = lax.dot_general(flat, factor, (((1,), (1,)), ((), ())), preferred_element_type=jnp.float32)
    px = px.reshape(acts.shape[0], acts.shape[1], factor.shape[0])
    feats = jnp.einsum('eas,esb->eab', grads.astype(jnp.float32), px, precision=lax.Precision.HIGHEST)
    return feats.reshape(acts.shape[0], -1) * (1.0 / math.sqrt(SEQ))

def reference(activations, grad_proj, proj_in):

    def one_layer(items):
        acts, grads, factor = items
        feats = layer_features(acts, grads, factor)
        return lax.dot_general(feats, feats, (((1,), (1,)), ((), ())), precision=lax.Precision.HIGHEST, preferred_element_type=jnp.float32)
    terms = lax.map(one_layer, (activations, grad_proj, proj_in))
    return lax.optimization_barrier(jnp.sum(terms, axis=0)) * (1.0 / math.sqrt(LAYERS * RANK * RANK))
```

```python
import math

import jax
import jax.numpy as jnp
from jax import lax
from jax.experimental import pallas as pl
from jax.experimental.pallas import tpu as pltpu
from jax.sharding import PartitionSpec as P

F32, BF16 = jnp.float32, jnp.bfloat16
LANES = 128
BLOCK = 1024
WINDOW = 3
Z_BITS = 1
VMEM_BYTES = 60 * 2**20
GRAM_VMEM = 8 * 2**20


def split3(x):
    high = x.astype(BF16)
    rest = x - high.astype(F32)
    mid = rest.astype(BF16)
    low = (rest - mid.astype(F32)).astype(BF16)
    return high, mid, low


def sum_blocks(product, rows, columns):
    total = None
    for order in (4, 3, 2, 1, 0):
        for i in range(3):
            j = order - i
            if 0 <= j < 3:
                block = product[i * rows : (i + 1) * rows, j * columns : (j + 1) * columns]
                total = block if total is None else total + block
    return total


def blocks_of(width):
    return [(at, min(BLOCK, width - at)) for at in range(0, width, BLOCK)]


def features_kernel(parts, acts, proj, grads, out, acts_buf, proj_buf, grads_buf, px, packed, acts_sem, proj_sem, grads_sem):
    count, rank, seq = grads.shape
    blocks = blocks_of(acts.shape[1])
    copies = []
    for n, (at, width) in enumerate(blocks):
        cut = pl.ds(at, width)
        copies.append((
            pltpu.make_async_copy(proj.at[:, cut], proj_buf.at[:, cut], proj_sem.at[n]),
            pltpu.make_async_copy(acts.at[:, cut], acts_buf.at[:, cut], acts_sem.at[n]),
        ))
    grads_copy = pltpu.make_async_copy(grads, grads_buf, grads_sem)
    for pair in copies[:WINDOW]:
        for copy in pair:
            copy.start()
    grads_copy.start()
    for n, (at, width) in enumerate(blocks):
        for copy in copies[n]:
            copy.wait()
        if n + WINDOW < len(blocks):
            for copy in copies[n + WINDOW]:
                copy.start()
        cut = pl.ds(at, width)
        term = lax.dot_general(
            acts_buf[:, cut], proj_buf[:, cut], (((1,), (1,)), ((), ())), preferred_element_type=F32
        )
        if n == 0:
            px[...] = term
        else:
            px[...] += term
    grads_copy.wait()
    half = rank // 2
    deep = half // parts
    for e in range(count):
        left = jnp.concatenate(split3(grads_buf[e]), axis=0)
        right = jnp.concatenate(split3(px[e * seq : (e + 1) * seq]), axis=1)
        feats = sum_blocks(jnp.dot(left, right, preferred_element_type=F32), rank, rank)
        feats = jnp.concatenate([feats[:half], feats[half:]], axis=1)
        for part in range(parts):
            packed[part, e * deep : (e + 1) * deep] = feats[part * deep : (part + 1) * deep]
    side = parts // 2
    for dest in range(out.shape[0]):
        part = dest // 16 * side + dest % side
        out[dest] = packed[part]


def features(parts, acts, proj, grads):
    count, rank, seq = grads.shape
    rows, width = acts.shape
    steps = len(blocks_of(width))
    deep = count * rank // 2 // parts
    anywhere = pl.BlockSpec(memory_space=pl.ANY)
    return pl.pallas_call(
        lambda *refs: features_kernel(parts, *refs),
        out_shape=jax.ShapeDtypeStruct((32, deep, 2 * rank), F32),
        in_specs=[anywhere] * 3,
        out_specs=pl.BlockSpec(memory_space=pltpu.VMEM),
        scratch_shapes=[
            pltpu.VMEM((rows, width), BF16),
            pltpu.VMEM((rank, width), BF16),
            pltpu.VMEM((count, rank, seq), F32),
            pltpu.VMEM((rows, rank), F32),
            pltpu.VMEM((parts, deep, 2 * rank), F32),
            pltpu.SemaphoreType.DMA((steps,)),
            pltpu.SemaphoreType.DMA((steps,)),
            pltpu.SemaphoreType.DMA,
        ],
        compiler_params=pltpu.CompilerParams(vmem_limit_bytes=VMEM_BYTES),
        name="features",
    )(acts, proj, grads)


def gram_kernel(parts, deep, feats, out, gram):
    examples = gram.shape[0]
    rows = jnp.concatenate(
        [feats[pl.ds(r, examples, stride=deep), :] for r in range(deep)], axis=1
    )
    terms = jnp.concatenate(split3(rows), axis=0)
    product = lax.dot_general(terms, terms, (((1,), (1,)), ((), ())), preferred_element_type=F32)
    gram[...] = sum_blocks(product, examples, examples)
    side = parts // 2
    group = lax.rem(lax.axis_index("ex"), 16) // side
    tall = 2 * side
    for x in range(2):
        mine = gram[pl.ds(x * 32 + group * tall, tall), :]
        for column in range(out.shape[0]):
            out[column, x * tall : (x + 1) * tall] = mine[:, column * 8 : (column + 1) * 8]


def gram_terms(parts, feats):
    sources, deep, lanes = feats.shape
    examples = 2 * sources
    return pl.pallas_call(
        lambda *refs: gram_kernel(parts, deep // 2, *refs),
        out_shape=jax.ShapeDtypeStruct((8, 2 * parts, 8), F32),
        in_specs=[pl.BlockSpec(memory_space=pltpu.VMEM)],
        out_specs=pl.BlockSpec(memory_space=pltpu.VMEM),
        scratch_shapes=[pltpu.VMEM((examples, examples), F32)],
        compiler_params=pltpu.CompilerParams(vmem_limit_bytes=GRAM_VMEM),
        name="gram_terms",
    )(feats.reshape(sources * deep, lanes))


def shards(activations, grad_proj, proj_in):
    _, count, seq, width = activations.shape
    rank = proj_in.shape[1]
    depth = lax.axis_size("layer")
    side = 2 << Z_BITS
    parts = 2 * side
    feats = features(parts, activations.reshape(count * seq, width), proj_in[0], grad_proj[0])
    feats = lax.all_to_all(feats, "ex", 0, 0, tiled=True)
    terms = gram_terms(parts, feats).reshape(8 * parts, 2, 8)
    groups = [
        [(x * 16 + z * side + w) * depth + layer for layer in range(depth) for x in range(2) for w in range(side)]
        for z in range(16 // side)
    ]
    terms = lax.all_to_all(terms, ("ex", "layer"), 0, 0, axis_index_groups=groups, tiled=True)
    return jnp.sum(terms, axis=0) * (1.0 / (seq * math.sqrt(depth * rank * rank)))


def solution(mesh):
    return jax.shard_map(
        shards,
        mesh=mesh,
        in_specs=(
            P("layer", "ex", None, None),
            P("layer", "ex", None, None),
            P("layer", None, None),
        ),
        out_specs=P("ex", "layer"),
        check_vma=False,
    )
```

```python
import math

import jax
import jax.numpy as jnp
import numpy as np
from jax import lax
from jax.experimental import pallas as pl
from jax.experimental.pallas import tpu as pltpu
from jax.sharding import PartitionSpec as P

F32, BF16 = jnp.float32, jnp.bfloat16
LANES = 128
FIRST, LARGE, LAST = 4, 16, (12, 6)
WINDOW = 7
Z_BITS = 1
VMEM_BYTES = 16 * 2**20
GRAM_VMEM = 8 * 2**20


def split3(x):
    high = x.astype(BF16)
    rest = x - high.astype(F32)
    mid = rest.astype(BF16)
    low = (rest - mid.astype(F32)).astype(BF16)
    return high, mid, low


def sum_blocks(product, rows, columns):
    total = None
    for order in (4, 3, 2, 1, 0):
        for i in range(3):
            j = order - i
            if 0 <= j < 3:
                block = product[i * rows : (i + 1) * rows, j * columns : (j + 1) * columns]
                total = block if total is None else total + block
    return total


def blocks_of(width):
    left = width // LANES - FIRST - sum(LAST)
    tiles = [FIRST] + [LARGE] * (left // LARGE) + [left % LARGE] * (left % LARGE > 0) + list(LAST)
    ends = np.cumsum(tiles) * LANES
    return [(int(end) - tile * LANES, tile * LANES) for end, tile in zip(ends, tiles)]


def features_kernel(parts, acts, proj, grads, out, acts_buf, proj_buf, grads_buf, px, packed, acts_sem, proj_sem, grads_sem):
    count, rank, seq = grads.shape
    blocks = blocks_of(acts.shape[1])
    copies = []
    for n, (at, width) in enumerate(blocks):
        cut = pl.ds(at, width)
        copies.append((
            pltpu.make_async_copy(proj.at[:, cut], proj_buf.at[:, cut], proj_sem.at[n]),
            pltpu.make_async_copy(acts.at[:, cut], acts_buf.at[:, cut], acts_sem.at[n]),
        ))
    grads_copy = pltpu.make_async_copy(grads, grads_buf, grads_sem)
    for pair in copies[:WINDOW]:
        for copy in pair:
            copy.start()
    grads_copy.start()
    for n, (at, width) in enumerate(blocks):
        for copy in copies[n]:
            copy.wait()
        if n + WINDOW < len(blocks):
            for copy in copies[n + WINDOW]:
                copy.start()
        cut = pl.ds(at, width)
        term = lax.dot_general(
            acts_buf[:, cut], proj_buf[:, cut], (((1,), (1,)), ((), ())), preferred_element_type=F32
        )
        if n == 0:
            px[...] = term
        else:
            px[...] += term
    grads_copy.wait()
    half = rank // 2
    deep = half // parts
    for e in range(count):
        left = jnp.concatenate(split3(grads_buf[e]), axis=0)
        right = jnp.concatenate(split3(px[e * seq : (e + 1) * seq]), axis=1)
        feats = sum_blocks(jnp.dot(left, right, preferred_element_type=F32), rank, rank)
        feats = jnp.concatenate([feats[:half], feats[half:]], axis=1)
        for part in range(parts):
            packed[part, e * deep : (e + 1) * deep] = feats[part * deep : (part + 1) * deep]
    side = parts // 2
    for dest in range(out.shape[0]):
        part = dest // 16 * side + dest % side
        out[dest] = packed[part]


def features(parts, acts, proj, grads):
    count, rank, seq = grads.shape
    rows, width = acts.shape
    steps = len(blocks_of(width))
    deep = count * rank // 2 // parts
    anywhere = pl.BlockSpec(memory_space=pl.ANY)
    return pl.pallas_call(
        lambda *refs: features_kernel(parts, *refs),
        out_shape=pltpu.VMEM((32, deep, 2 * rank), F32),
        in_specs=[anywhere] * 3,
        out_specs=pl.BlockSpec(memory_space=pltpu.VMEM),
        scratch_shapes=[
            pltpu.VMEM((rows, width), BF16),
            pltpu.VMEM((rank, width), BF16),
            pltpu.VMEM((count, rank, seq), F32),
            pltpu.VMEM((rows, rank), F32),
            pltpu.VMEM((parts, deep, 2 * rank), F32),
            pltpu.SemaphoreType.DMA((steps,)),
            pltpu.SemaphoreType.DMA((steps,)),
            pltpu.SemaphoreType.DMA,
        ],
        compiler_params=pltpu.CompilerParams(vmem_limit_bytes=VMEM_BYTES),
        name="features",
    )(*(pltpu.with_memory_space_constraint(x, pltpu.HBM) for x in (acts, proj, grads)))


def gram_kernel(parts, deep, scale, feats, out, gram):
    examples = gram.shape[0]
    rows = jnp.concatenate(
        [feats[pl.ds(r, examples, stride=deep), :] for r in range(deep)], axis=1
    )
    terms = jnp.concatenate(split3(rows), axis=0)
    product = lax.dot_general(terms, terms, (((1,), (1,)), ((), ())), preferred_element_type=F32)
    gram[...] = sum_blocks(product, examples, examples) * scale
    side = parts // 2
    group = lax.rem(lax.axis_index("ex"), 16) // side
    tall = 2 * side
    for x in range(2):
        mine = gram[pl.ds(x * 32 + group * tall, tall), :]
        for column in range(out.shape[0]):
            out[column, x * tall : (x + 1) * tall] = mine[:, column * 8 : (column + 1) * 8]


def gram_terms(parts, scale, feats):
    sources, deep, lanes = feats.shape
    examples = 2 * sources
    return pl.pallas_call(
        lambda *refs: gram_kernel(parts, deep // 2, scale, *refs),
        out_shape=jax.ShapeDtypeStruct((8, 2 * parts, 8), F32),
        in_specs=[pl.BlockSpec(memory_space=pltpu.VMEM)],
        out_specs=pl.BlockSpec(memory_space=pltpu.VMEM),
        scratch_shapes=[pltpu.VMEM((examples, examples), F32)],
        compiler_params=pltpu.CompilerParams(vmem_limit_bytes=GRAM_VMEM),
        name="gram_terms",
    )(feats.reshape(sources * deep, lanes))


def shards(activations, grad_proj, proj_in):
    _, count, seq, width = activations.shape
    rank = proj_in.shape[1]
    depth = lax.axis_size("layer")
    side = 2 << Z_BITS
    parts = 2 * side
    feats = features(parts, activations.reshape(count * seq, width), proj_in[0], grad_proj[0])
    feats = lax.all_to_all(feats, "ex", 0, 0, tiled=True)
    scale = 1.0 / (seq * math.sqrt(depth * rank * rank))
    terms = gram_terms(parts, scale, feats).reshape(8 * parts, 2, 8)
    groups = [
        [(x * 16 + z * side + w) * depth + layer for layer in range(depth) for x in range(2) for w in range(side)]
        for z in range(16 // side)
    ]
    terms = lax.all_to_all(terms, ("ex", "layer"), 0, 0, axis_index_groups=groups, tiled=True)
    return jnp.sum(terms, axis=0)


def solution(mesh):
    return jax.shard_map(
        shards,
        mesh=mesh,
        in_specs=(
            P("layer", "ex", None, None),
            P("layer", "ex", None, None),
            P("layer", None, None),
        ),
        out_specs=P("ex", "layer"),
        check_vma=False,
    )
```

```python
import math

import jax
import jax.numpy as jnp
import numpy as np
from jax import lax
from jax.experimental import pallas as pl
from jax.experimental.pallas import tpu as pltpu
from jax.sharding import PartitionSpec as P

F32, BF16 = jnp.float32, jnp.bfloat16
LANES = 128
FIRST, LARGE, LAST = 4, 16, (12, 6)
WINDOW = 7
Z_BITS = 1
VMEM_BYTES = 16 * 2**20
GRAM_VMEM = 8 * 2**20


def first_order():
    return list(reversed(range(32)))


def second_order(parts):
    return [(layer, part) for layer in reversed(range(8)) for part in reversed(range(parts))]


def split3(x):
    high = x.astype(BF16)
    rest = x - high.astype(F32)
    mid = rest.astype(BF16)
    low = (rest - mid.astype(F32)).astype(BF16)
    return high, mid, low


def sum_blocks(product, rows, columns):
    total = None
    for order in (4, 3, 2, 1, 0):
        for i in range(3):
            j = order - i
            if 0 <= j < 3:
                block = product[i * rows : (i + 1) * rows, j * columns : (j + 1) * columns]
                total = block if total is None else total + block
    return total


def blocks_of(width):
    left = width // LANES - FIRST - sum(LAST)
    tiles = [FIRST] + [LARGE] * (left // LARGE) + [left % LARGE] * (left % LARGE > 0) + list(LAST)
    ends = np.cumsum(tiles) * LANES
    return [(int(end) - tile * LANES, tile * LANES) for end, tile in zip(ends, tiles)]


def product_of(left, right):
    return lax.dot_general(left, right, (((1,), (1,)), ((), ())), preferred_element_type=F32)


def features_kernel(parts, acts, proj, grads, out, acts_buf, proj_buf, grads_buf, px, px_t, packed, acts_sem, proj_sem, grads_sem):
    count, rank, seq = grads.shape
    blocks = blocks_of(acts.shape[1])
    copies = []
    for n, (at, width) in enumerate(blocks):
        cut = pl.ds(at, width)
        copies.append((
            pltpu.make_async_copy(proj.at[:, cut], proj_buf.at[:, cut], proj_sem.at[n]),
            pltpu.make_async_copy(acts.at[:, cut], acts_buf.at[:, cut], acts_sem.at[n]),
        ))
    grads_copy = pltpu.make_async_copy(grads, grads_buf, grads_sem)
    for n, pair in enumerate(copies[:WINDOW]):
        for copy in pair:
            copy.start()
        if n == 1:
            grads_copy.start()
    for n, (at, width) in enumerate(blocks):
        for copy in copies[n]:
            copy.wait()
        if n + WINDOW < len(blocks):
            for copy in copies[n + WINDOW]:
                copy.start()
        cut = pl.ds(at, width)
        first, second = acts_buf[:seq, cut], acts_buf[seq:, cut]
        weights = proj_buf[:, cut]
        terms = product_of(first, weights), product_of(weights, second)
        for total, term in zip((px, px_t), terms):
            if n == 0:
                total[...] = term
            else:
                total[...] += term
    grads_copy.wait()
    half = rank // 2
    deep = half // parts
    for e in range(count):
        left = jnp.concatenate(split3(grads_buf[e]), axis=0)
        if e == 0:
            product = jnp.dot(left, jnp.concatenate(split3(px[...]), axis=1), preferred_element_type=F32)
        else:
            product = product_of(left, jnp.concatenate(split3(px_t[...]), axis=0))
        feats = sum_blocks(product, rank, rank)
        feats = jnp.concatenate([feats[:half], feats[half:]], axis=1)
        for part in range(parts):
            packed[part, e * deep : (e + 1) * deep] = feats[part * deep : (part + 1) * deep]
    side = parts // 2
    for rank_in_group, dest in enumerate(first_order()):
        part = dest // 16 * side + dest % side
        out[rank_in_group] = packed[part]


def features(parts, acts, proj, grads):
    count, rank, seq = grads.shape
    rows, width = acts.shape
    steps = len(blocks_of(width))
    deep = count * rank // 2 // parts
    anywhere = pl.BlockSpec(memory_space=pl.ANY)
    return pl.pallas_call(
        lambda *refs: features_kernel(parts, *refs),
        out_shape=pltpu.VMEM((32, deep, 2 * rank), F32),
        in_specs=[anywhere] * 3,
        out_specs=pl.BlockSpec(memory_space=pltpu.VMEM),
        scratch_shapes=[
            pltpu.VMEM((rows, width), BF16),
            pltpu.VMEM((rank, width), BF16),
            pltpu.VMEM((count, rank, seq), F32),
            pltpu.VMEM((seq, rank), F32),
            pltpu.VMEM((rank, seq), F32),
            pltpu.VMEM((parts, deep, 2 * rank), F32),
            pltpu.SemaphoreType.DMA((steps,)),
            pltpu.SemaphoreType.DMA((steps,)),
            pltpu.SemaphoreType.DMA,
        ],
        compiler_params=pltpu.CompilerParams(vmem_limit_bytes=VMEM_BYTES),
        name="features",
    )(*(pltpu.with_memory_space_constraint(x, pltpu.HBM) for x in (acts, proj, grads)))


def gram_kernel(parts, deep, scale, received, out, feats, gram):
    examples = gram.shape[0]
    tile = 2 * deep
    for rank_in_group, source in enumerate(first_order()):
        feats[source * tile : (source + 1) * tile] = received[rank_in_group * tile : (rank_in_group + 1) * tile]
    rows = jnp.concatenate(
        [feats[pl.ds(r, examples, stride=deep), :] for r in range(deep)], axis=1
    )
    terms = jnp.concatenate(split3(rows), axis=0)
    product = lax.dot_general(terms, terms, (((1,), (1,)), ((), ())), preferred_element_type=F32)
    gram[...] = sum_blocks(product, examples, examples) * scale
    side = parts // 2
    group = lax.rem(lax.axis_index("ex"), 16) // side
    tall = 2 * side
    mine = jnp.concatenate(
        [gram[pl.ds(x * 32 + group * tall, tall), :] for x in range(2)], axis=0
    )
    columns = [mine[:, layer * 8 : (layer + 1) * 8] for layer in range(8)]
    for rank_in_group, (layer, part) in enumerate(second_order(parts)):
        out[2 * rank_in_group : 2 * rank_in_group + 2] = columns[layer][2 * part : 2 * part + 2]


def gram_terms(parts, scale, feats):
    sources, deep, lanes = feats.shape
    examples = 2 * sources
    return pl.pallas_call(
        lambda *refs: gram_kernel(parts, deep // 2, scale, *refs),
        out_shape=jax.ShapeDtypeStruct((16 * parts, 8), F32),
        in_specs=[pl.BlockSpec(memory_space=pltpu.VMEM)],
        out_specs=pl.BlockSpec(memory_space=pltpu.VMEM),
        scratch_shapes=[pltpu.VMEM((sources * deep, lanes), F32), pltpu.VMEM((examples, examples), F32)],
        compiler_params=pltpu.CompilerParams(vmem_limit_bytes=GRAM_VMEM),
        name="gram_terms",
    )(feats.reshape(sources * deep, lanes))


def shards(activations, grad_proj, proj_in):
    _, count, seq, width = activations.shape
    rank = proj_in.shape[1]
    depth = lax.axis_size("layer")
    side = 2 << Z_BITS
    parts = 2 * side
    feats = features(parts, activations.reshape(count * seq, width), proj_in[0], grad_proj[0])
    feats = lax.all_to_all(feats, "ex", 0, 0, axis_index_groups=[first_order()], tiled=True)
    scale = 1.0 / (seq * math.sqrt(depth * rank * rank))
    terms = gram_terms(parts, scale, feats).reshape(8 * parts, 2, 8)
    groups = [
        [(part // side * 16 + z * side + part % side) * depth + layer for layer, part in second_order(parts)]
        for z in range(16 // side)
    ]
    terms = lax.all_to_all(terms, ("ex", "layer"), 0, 0, axis_index_groups=groups, tiled=True)
    return jnp.sum(terms, axis=0)


def solution(mesh):
    return jax.shard_map(
        shards,
        mesh=mesh,
        in_specs=(
            P("layer", "ex", None, None),
            P("layer", "ex", None, None),
            P("layer", None, None),
        ),
        out_specs=P("ex", "layer"),
        check_vma=False,
    )
```

```python
import math

import jax
import jax.numpy as jnp
import numpy as np
from jax import lax
from jax.experimental import pallas as pl
from jax.experimental.pallas import tpu as pltpu
from jax.sharding import PartitionSpec as P

F32, BF16 = jnp.float32, jnp.bfloat16
LANES = 128
FIRST, LARGE, LAST = 4, 16, (12, 6)
WINDOW = 7
Z_BITS = 1
VMEM_BYTES = 16 * 2**20
GRAM_VMEM = 8 * 2**20


def first_order():
    return [x * 16 + z * 2 + core for z in (4, 5, 6, 7, 0, 1, 2, 3) for x in (1, 0) for core in (1, 0)]


def second_order(parts):
    return [(layer, part) for layer in (6, 7, 5, 4, 2, 3, 1, 0) for part in reversed(range(parts))]


def split3(x):
    high = x.astype(BF16)
    rest = x - high.astype(F32)
    mid = rest.astype(BF16)
    low = (rest - mid.astype(F32)).astype(BF16)
    return high, mid, low


def sum_blocks(product, rows, columns):
    total = None
    for order in (4, 3, 2, 1, 0):
        for i in range(3):
            j = order - i
            if 0 <= j < 3:
                block = product[i * rows : (i + 1) * rows, j * columns : (j + 1) * columns]
                total = block if total is None else total + block
    return total


def blocks_of(width):
    left = width // LANES - FIRST - sum(LAST)
    tiles = [FIRST] + [LARGE] * (left // LARGE) + [left % LARGE] * (left % LARGE > 0) + list(LAST)
    ends = np.cumsum(tiles) * LANES
    return [(int(end) - tile * LANES, tile * LANES) for end, tile in zip(ends, tiles)]


def product_of(left, right):
    return lax.dot_general(left, right, (((1,), (1,)), ((), ())), preferred_element_type=F32)


def features_kernel(parts, acts, proj, grads, out, acts_buf, proj_buf, grads_buf, px, px_t, packed, acts_sem, proj_sem, grads_sem):
    count, rank, seq = grads.shape
    blocks = blocks_of(acts.shape[1])
    copies = []
    for n, (at, width) in enumerate(blocks):
        cut = pl.ds(at, width)
        copies.append((
            pltpu.make_async_copy(proj.at[:, cut], proj_buf.at[:, cut], proj_sem.at[n]),
            pltpu.make_async_copy(acts.at[:, cut], acts_buf.at[:, cut], acts_sem.at[n]),
        ))
    grads_copy = pltpu.make_async_copy(grads, grads_buf, grads_sem)
    for n, pair in enumerate(copies[:WINDOW]):
        for copy in pair:
            copy.start()
        if n == 1:
            grads_copy.start()
    for n, (at, width) in enumerate(blocks):
        for copy in copies[n]:
            copy.wait()
        if n + WINDOW < len(blocks):
            for copy in copies[n + WINDOW]:
                copy.start()
        cut = pl.ds(at, width)
        first, second = acts_buf[:seq, cut], acts_buf[seq:, cut]
        weights = proj_buf[:, cut]
        terms = product_of(first, weights), product_of(weights, second)
        for total, term in zip((px, px_t), terms):
            if n == 0:
                total[...] = term
            else:
                total[...] += term
    grads_copy.wait()
    half = rank // 2
    deep = half // parts
    for e in range(count):
        left = jnp.concatenate(split3(grads_buf[e]), axis=0)
        if e == 0:
            product = jnp.dot(left, jnp.concatenate(split3(px[...]), axis=1), preferred_element_type=F32)
        else:
            product = product_of(left, jnp.concatenate(split3(px_t[...]), axis=0))
        feats = sum_blocks(product, rank, rank)
        feats = jnp.concatenate([feats[:half], feats[half:]], axis=1)
        for part in range(parts):
            packed[part, e * deep : (e + 1) * deep] = feats[part * deep : (part + 1) * deep]
    side = parts // 2
    for rank_in_group, dest in enumerate(first_order()):
        part = dest // 16 * side + dest % side
        out[rank_in_group] = packed[part]


def features(parts, acts, proj, grads):
    count, rank, seq = grads.shape
    rows, width = acts.shape
    steps = len(blocks_of(width))
    deep = count * rank // 2 // parts
    anywhere = pl.BlockSpec(memory_space=pl.ANY)
    return pl.pallas_call(
        lambda *refs: features_kernel(parts, *refs),
        out_shape=pltpu.VMEM((32, deep, 2 * rank), F32),
        in_specs=[anywhere] * 3,
        out_specs=pl.BlockSpec(memory_space=pltpu.VMEM),
        scratch_shapes=[
            pltpu.VMEM((rows, width), BF16),
            pltpu.VMEM((rank, width), BF16),
            pltpu.VMEM((count, rank, seq), F32),
            pltpu.VMEM((seq, rank), F32),
            pltpu.VMEM((rank, seq), F32),
            pltpu.VMEM((parts, deep, 2 * rank), F32),
            pltpu.SemaphoreType.DMA((steps,)),
            pltpu.SemaphoreType.DMA((steps,)),
            pltpu.SemaphoreType.DMA,
        ],
        compiler_params=pltpu.CompilerParams(vmem_limit_bytes=VMEM_BYTES),
        name="features",
    )(*(pltpu.with_memory_space_constraint(x, pltpu.HBM) for x in (acts, proj, grads)))


def gram_kernel(parts, deep, scale, received, out, feats, gram):
    examples = gram.shape[0]
    tile = 2 * deep
    for rank_in_group, source in enumerate(first_order()):
        feats[source * tile : (source + 1) * tile] = received[rank_in_group * tile : (rank_in_group + 1) * tile]
    rows = jnp.concatenate(
        [feats[pl.ds(r, examples, stride=deep), :] for r in range(deep)], axis=1
    )
    terms = jnp.concatenate(split3(rows), axis=0)
    product = lax.dot_general(terms, terms, (((1,), (1,)), ((), ())), preferred_element_type=F32)
    gram[...] = sum_blocks(product, examples, examples) * scale
    side = parts // 2
    group = lax.rem(lax.axis_index("ex"), 16) // side
    tall = 2 * side
    mine = jnp.concatenate(
        [gram[pl.ds(x * 32 + group * tall, tall), :] for x in range(2)], axis=0
    )
    columns = [mine[:, layer * 8 : (layer + 1) * 8] for layer in range(8)]
    for rank_in_group, (layer, part) in enumerate(second_order(parts)):
        out[2 * rank_in_group : 2 * rank_in_group + 2] = columns[layer][2 * part : 2 * part + 2]


def gram_terms(parts, scale, feats):
    sources, deep, lanes = feats.shape
    examples = 2 * sources
    return pl.pallas_call(
        lambda *refs: gram_kernel(parts, deep // 2, scale, *refs),
        out_shape=jax.ShapeDtypeStruct((16 * parts, 8), F32),
        in_specs=[pl.BlockSpec(memory_space=pltpu.VMEM)],
        out_specs=pl.BlockSpec(memory_space=pltpu.VMEM),
        scratch_shapes=[pltpu.VMEM((sources * deep, lanes), F32), pltpu.VMEM((examples, examples), F32)],
        compiler_params=pltpu.CompilerParams(vmem_limit_bytes=GRAM_VMEM),
        name="gram_terms",
    )(feats.reshape(sources * deep, lanes))


def shards(activations, grad_proj, proj_in):
    _, count, seq, width = activations.shape
    rank = proj_in.shape[1]
    depth = lax.axis_size("layer")
    side = 2 << Z_BITS
    parts = 2 * side
    feats = features(parts, activations.reshape(count * seq, width), proj_in[0], grad_proj[0])
    feats = lax.all_to_all(feats, "ex", 0, 0, axis_index_groups=[first_order()], tiled=True)
    scale = 1.0 / (seq * math.sqrt(depth * rank * rank))
    terms = gram_terms(parts, scale, feats).reshape(8 * parts, 2, 8)
    groups = [
        [(part // side * 16 + z * side + part % side) * depth + layer for layer, part in second_order(parts)]
        for z in range(16 // side)
    ]
    terms = lax.all_to_all(terms, ("ex", "layer"), 0, 0, axis_index_groups=groups, tiled=True)
    return jnp.sum(terms, axis=0)


def solution(mesh):
    return jax.shard_map(
        shards,
        mesh=mesh,
        in_specs=(
            P("layer", "ex", None, None),
            P("layer", "ex", None, None),
            P("layer", None, None),
        ),
        out_specs=P("ex", "layer"),
        check_vma=False,
    )
```

```python
import math

import jax
import jax.numpy as jnp
import numpy as np
from jax import lax
from jax.experimental import pallas as pl
from jax.experimental.pallas import tpu as pltpu
from jax.sharding import PartitionSpec as P

F32, BF16 = jnp.float32, jnp.bfloat16
LANES = 128
FIRST, LARGE, LAST = 4, 16, (12, 6)
WINDOW = 7
Z_BITS = 1
VMEM_BYTES = 16 * 2**20
GRAM_VMEM = 8 * 2**20


def first_order():
    return [x * 16 + z * 2 + core for z in (4, 5, 6, 7, 0, 1, 2, 3) for x in (1, 0) for core in (1, 0)]


def second_order(parts):
    return [(layer, part) for layer in (6, 7, 5, 4, 2, 3, 1, 0) for part in reversed(range(parts))]


def split3(x):
    high = x.astype(BF16)
    rest = x - high.astype(F32)
    mid = rest.astype(BF16)
    low = (rest - mid.astype(F32)).astype(BF16)
    return high, mid, low


def sum_blocks(product, rows, columns):
    total = None
    for order in (4, 3, 2, 1, 0):
        for i in range(3):
            j = order - i
            if 0 <= j < 3:
                block = product[i * rows : (i + 1) * rows, j * columns : (j + 1) * columns]
                total = block if total is None else total + block
    return total


def blocks_of(width):
    left = width // LANES - FIRST - sum(LAST)
    tiles = [FIRST] + [LARGE] * (left // LARGE) + [left % LARGE] * (left % LARGE > 0) + list(LAST)
    ends = np.cumsum(tiles) * LANES
    return [(int(end) - tile * LANES, tile * LANES) for end, tile in zip(ends, tiles)]


def product_of(left, right):
    return lax.dot_general(left, right, (((1,), (1,)), ((), ())), preferred_element_type=F32)


def features_kernel(parts, acts, proj, grads, out, acts_buf, proj_buf, grads_buf, px, px_t, packed, acts_sem, proj_sem, grads_sem):
    count, rank, seq = grads.shape
    blocks = blocks_of(acts.shape[1])
    copies = []
    for n, (at, width) in enumerate(blocks):
        cut = pl.ds(at, width)
        copies.append((
            pltpu.make_async_copy(proj.at[:, cut], proj_buf.at[:, cut], proj_sem.at[n]),
            pltpu.make_async_copy(acts.at[:, cut], acts_buf.at[:, cut], acts_sem.at[n]),
        ))
    grads_copy = pltpu.make_async_copy(grads, grads_buf, grads_sem)
    for n, pair in enumerate(copies[:WINDOW]):
        for copy in pair:
            copy.start()
        if n == 1:
            grads_copy.start()
    for n, (at, width) in enumerate(blocks):
        for copy in copies[n]:
            copy.wait()
        if n + WINDOW < len(blocks):
            for copy in copies[n + WINDOW]:
                copy.start()
        cut = pl.ds(at, width)
        first, second = acts_buf[:seq, cut], acts_buf[seq:, cut]
        weights = proj_buf[:, cut]
        terms = product_of(first, weights), product_of(weights, second)
        for total, term in zip((px, px_t), terms):
            if n == 0:
                total[...] = term
            else:
                total[...] += term
    grads_copy.wait()
    half = rank // 2
    deep = half // parts
    for e in range(count):
        left = jnp.concatenate(split3(grads_buf[e]), axis=0)
        if e == 0:
            product = jnp.dot(left, jnp.concatenate(split3(px[...]), axis=1), preferred_element_type=F32)
        else:
            product = product_of(left, jnp.concatenate(split3(px_t[...]), axis=0))
        feats = sum_blocks(product, rank, rank)
        feats = jnp.concatenate([feats[:half], feats[half:]], axis=1)
        for part in range(parts):
            packed[part, e * deep : (e + 1) * deep] = feats[part * deep : (part + 1) * deep]
    side = parts // 2
    for rank_in_group, dest in enumerate(first_order()):
        part = dest // 16 * side + dest % side
        out[rank_in_group] = packed[part]


def features(parts, acts, proj, grads):
    count, rank, seq = grads.shape
    rows, width = acts.shape
    steps = len(blocks_of(width))
    deep = count * rank // 2 // parts
    anywhere = pl.BlockSpec(memory_space=pl.ANY)
    return pl.pallas_call(
        lambda *refs: features_kernel(parts, *refs),
        out_shape=pltpu.VMEM((32, deep, 2 * rank), F32),
        in_specs=[anywhere] * 3,
        out_specs=pl.BlockSpec(memory_space=pltpu.VMEM),
        scratch_shapes=[
            pltpu.VMEM((rows, width), BF16),
            pltpu.VMEM((rank, width), BF16),
            pltpu.VMEM((count, rank, seq), F32),
            pltpu.VMEM((seq, rank), F32),
            pltpu.VMEM((rank, seq), F32),
            pltpu.VMEM((parts, deep, 2 * rank), F32),
            pltpu.SemaphoreType.DMA((steps,)),
            pltpu.SemaphoreType.DMA((steps,)),
            pltpu.SemaphoreType.DMA,
        ],
        compiler_params=pltpu.CompilerParams(vmem_limit_bytes=VMEM_BYTES),
        name="features",
    )(*(pltpu.with_memory_space_constraint(x, pltpu.HBM) for x in (acts, proj, grads)))


def gram_kernel(parts, deep, scale, received, out, feats, examples_by_share):
    examples = examples_by_share.shape[0]
    tile = 2 * deep
    for rank_in_group, source in enumerate(first_order()):
        feats[source * tile : (source + 1) * tile] = received[rank_in_group * tile : (rank_in_group + 1) * tile]
    rows = jnp.concatenate(
        [feats[pl.ds(r, examples, stride=deep), :] for r in range(deep)], axis=1
    )
    examples_by_share[...] = rows
    side = parts // 2
    group = lax.rem(lax.axis_index("ex"), 16) // side
    tall = 2 * side
    mine = jnp.concatenate(
        [examples_by_share[pl.ds(x * 32 + group * tall, tall), :] for x in range(2)], axis=0
    )
    left = jnp.concatenate(split3(mine), axis=0)
    right = jnp.concatenate(split3(rows), axis=0)
    mine = sum_blocks(product_of(left, right), 2 * tall, examples) * scale
    columns = [mine[:, layer * 8 : (layer + 1) * 8] for layer in range(8)]
    for rank_in_group, (layer, part) in enumerate(second_order(parts)):
        out[2 * rank_in_group : 2 * rank_in_group + 2] = columns[layer][2 * part : 2 * part + 2]


def gram_terms(parts, scale, feats):
    sources, deep, lanes = feats.shape
    examples = 2 * sources
    return pl.pallas_call(
        lambda *refs: gram_kernel(parts, deep // 2, scale, *refs),
        out_shape=jax.ShapeDtypeStruct((16 * parts, 8), F32),
        in_specs=[pl.BlockSpec(memory_space=pltpu.VMEM)],
        out_specs=pl.BlockSpec(memory_space=pltpu.VMEM),
        scratch_shapes=[pltpu.VMEM((sources * deep, lanes), F32), pltpu.VMEM((examples, deep // 2 * lanes), F32)],
        compiler_params=pltpu.CompilerParams(vmem_limit_bytes=GRAM_VMEM),
        name="gram_terms",
    )(feats.reshape(sources * deep, lanes))


def shards(activations, grad_proj, proj_in):
    _, count, seq, width = activations.shape
    rank = proj_in.shape[1]
    depth = lax.axis_size("layer")
    side = 2 << Z_BITS
    parts = 2 * side
    feats = features(parts, activations.reshape(count * seq, width), proj_in[0], grad_proj[0])
    feats = lax.all_to_all(feats, "ex", 0, 0, axis_index_groups=[first_order()], tiled=True)
    scale = 1.0 / (seq * math.sqrt(depth * rank * rank))
    terms = gram_terms(parts, scale, feats).reshape(8 * parts, 2, 8)
    groups = [
        [(part // side * 16 + z * side + part % side) * depth + layer for layer, part in second_order(parts)]
        for z in range(16 // side)
    ]
    terms = lax.all_to_all(terms, ("ex", "layer"), 0, 0, axis_index_groups=groups, tiled=True)
    return jnp.sum(terms, axis=0)


def solution(mesh):
    return jax.shard_map(
        shards,
        mesh=mesh,
        in_specs=(
            P("layer", "ex", None, None),
            P("layer", "ex", None, None),
            P("layer", None, None),
        ),
        out_specs=P("ex", "layer"),
        check_vma=False,
    )
```
